32 devices in a mesh: row: 4 (over x, core), col: 8 (over z, y).
Axes of the slice: x: 2, y: 2, z: 4, core: 2. Of those that a mesh axis runs over, the one named last changes fastest.
Arguments:
- right_side: float32 [32768, 128], P(('row', 'col')), may hold values from -6 to 6
- leaf_inverse: bfloat16 [32768, 1024], P(('row', 'col')), may hold values from -0.1875 to 0.1875
- compress: bfloat16 [32768, 1024], P(('row', 'col')), may hold values from -0.1875 to 0.1875
- middle: bfloat16 [32768, 1024], P(('row', 'col')), may hold values from -0.1875 to 0.1875
- expand: bfloat16 [32768, 1024], P(('row', 'col')), may hold values from -0.1875 to 0.1875
- row_project: bfloat16 [2, 32768, 256], P(None, ('row', 'col')), may hold values from -0.1875 to 0.1875
- row_expand: bfloat16 [2, 32768, 256], P(None, ('row', 'col')), may hold values from -0.25 to 0.25
- root_project: bfloat16 [32768, 256], P(('row', 'col')), may hold values from -0.03125 to 0.03125
- root_expand: bfloat16 [32768, 256], P(('row', 'col')), may hold values from -0.375 to 0.375
- owner_map: int32 [8], replicated, may hold values from 0 to 7, each once
Outputs:
- applied: float32 [32768, 128], P(('row', 'col'))
The draws below stay inside these ranges and needn't reach their ends.
Inputs may be any that keep to these rules, and one draw needn't show every extreme that they name: owner_map names each of the 8 column positions exactly once.
All inputs are finite; a program needn't handle non-finite values.
Results may differ from the reference program's by a relative error of at most 0.004.
Values may be sent and summed in bfloat16 or wider, within the bound.
No kernel may reach another device: no remote copies, remote signals or barrier semaphores. Data moves between devices by JAX's collectives and lax.ppermute only.
A program may use at most 128 MiB of HBM per device.

```python
import jax
import jax.numpy as jnp
from jax import lax

LEAF = 1024
W = 128
S = 128
RANK = 256
LEVELS = 2
N = 32768
N_ROW = 4
N_COL = 8
DEVICES = 32


def block_scale(stream_key, dims, split, least, high):
    level = 1.0
    for dim, parts in split:
        heights = jax.random.uniform(jax.random.fold_in(jax.random.fold_in(stream_key, 6), dim), (parts,), jnp.float32, least / len(split), high / len(split))
        level = level * jnp.repeat(jnp.exp(heights), dims[dim] // parts).reshape((-1,) + (1,) * (len(dims) - 1 - dim))
    return level


def centred(rng, dims, scale, bound, cuts=(), held_as=jnp.bfloat16):
    drawn = jax.random.normal(rng, dims, jnp.float32) * scale
    if len(cuts) > 0:
        drawn = block_scale(rng, dims, cuts, -0.22, 0.18) * drawn
    return jnp.clip(drawn, min=-bound, max=bound).astype(held_as)


def setup_inputs(seed: int = 0) -> dict:
    streams_of = jax.random.split(jax.random.key(seed), 11)
    right_side = centred(streams_of[0], (N, W), 1.0, 6.0, ((0, 32),), jnp.float32)
    leaf_inverse = centred(streams_of[1], (N, LEAF), LEAF ** -0.5, 0.1875, ((0, 32),))
    compress = centred(streams_of[2], (N, N_COL * S), LEAF ** -0.5, 0.1875, ((0, 32),))
    middle = centred(streams_of[3], (N_ROW * N_COL * N_COL * S, N_COL * S), (N_COL * S) ** -0.5, 0.1875, ((0, 32),))
    expand = centred(streams_of[4], (N, N_COL * S), (N_COL * S) ** -0.5, 0.1875, ((0, 32),))
    row_project = centred(streams_of[5], (LEVELS, N, RANK), LEAF ** -0.5, 0.1875, ((1, 32),))
    row_expand = centred(streams_of[6], (LEVELS, N, RANK), (2 * RANK) ** -0.5, 0.25, ((1, 32),))
    root_project = centred(streams_of[7], (N, RANK), (LEAF * DEVICES) ** -0.5, 0.03125, ((0, 32),))
    root_expand = centred(streams_of[8], (N, RANK), RANK ** -0.5, 0.375, ((0, 32),))
    owner_map = jax.random.permutation(streams_of[9], N_COL).astype(jnp.int32)
    return dict(right_side=right_side, leaf_inverse=leaf_inverse, compress=compress, middle=middle, expand=expand, row_project=row_project, row_expand=row_expand, root_project=root_project, root_expand=root_expand, owner_map=owner_map)


def reference(right_side, leaf_inverse, compress, middle, expand, row_project, row_expand, root_project, root_expand, owner_map):
    leaves = N_ROW * N_COL
    block_rows = N_COL * S
    lowered = right_side.astype(jnp.bfloat16).reshape(leaves, LEAF, W)
    inverse_blocks = leaf_inverse.reshape(leaves, LEAF, LEAF)
    compress_blocks = compress.reshape(leaves, LEAF, block_rows)
    middle_blocks = middle.reshape(leaves, block_rows, block_rows)
    expand_blocks = expand.reshape(leaves, LEAF, block_rows)
    project_blocks = jnp.transpose(row_project.reshape(LEVELS, leaves, LEAF, RANK), (1, 0, 2, 3))
    expand_levels = jnp.transpose(row_expand.reshape(LEVELS, leaves, LEAF, RANK), (1, 0, 2, 3))
    root_in = root_project.reshape(leaves, LEAF, RANK)
    root_out = root_expand.reshape(leaves, LEAF, RANK)

    def leaf_work(operands):
        block, inverse_block, compress_block, project_block, root_block = operands
        dense_part = jnp.dot(inverse_block, block, preferred_element_type=jnp.float32)
        coeffs = jnp.dot(compress_block.T, block, preferred_element_type=jnp.float32).astype(jnp.bfloat16)
        level_coeffs = jnp.einsum("blr,lw->brw", project_block.astype(jnp.float32), block.astype(jnp.float32))
        root_term = jnp.dot(root_block.T, block, preferred_element_type=jnp.float32)
        return dense_part, coeffs, level_coeffs, root_term

    dense_part, coeffs, level_coeffs, root_term = lax.map(leaf_work, (lowered, inverse_blocks, compress_blocks, project_blocks, root_in))

    inverse = jnp.argsort(owner_map)
    by_source = coeffs.reshape(N_ROW, N_COL, N_COL, S, W)
    arrived = jnp.transpose(jnp.take(by_source, inverse, axis=2), (0, 2, 1, 3, 4)).reshape(leaves, block_rows, W)

    def mix_work(operands):
        return jnp.dot(operands[0], operands[1], preferred_element_type=jnp.float32).astype(jnp.bfloat16)

    mixed = lax.map(mix_work, (middle_blocks, arrived))
    by_owner = mixed.reshape(N_ROW, N_COL, N_COL, S, W)
    returned = jnp.transpose(jnp.take(by_owner, owner_map, axis=1), (0, 2, 1, 3, 4)).reshape(leaves, block_rows, W)

    def expand_work(operands):
        return jnp.dot(operands[0], operands[1], preferred_element_type=jnp.float32)

    cluster_part = lax.map(expand_work, (expand_blocks, returned))

    grid = level_coeffs.reshape(N_ROW, N_COL, LEVELS, RANK, W)
    sibling_list = []
    for level_bit in range(LEVELS):
        span = 2 ** level_bit
        pairs = N_ROW // (2 * span)
        grouped = grid[:, :, level_bit].reshape(pairs, 2, span, N_COL, RANK, W).sum(axis=2)
        swapped = grouped[:, ::-1]
        spread = jnp.broadcast_to(swapped[:, :, None], (pairs, 2, span, N_COL, RANK, W)).reshape(N_ROW, N_COL, RANK, W)
        sibling_list.append(spread)
    sibling = jnp.stack(sibling_list, axis=2).reshape(leaves, LEVELS, RANK, W).astype(jnp.bfloat16)
    root_coeffs = jnp.sum(root_term, axis=0).astype(jnp.bfloat16)

    def finish_work(operands):
        expand_block, sibling_block, root_block = operands
        coupled = jnp.einsum("blr,brw->lw", expand_block.astype(jnp.float32), sibling_block.astype(jnp.float32))
        root_part = jnp.dot(root_block, root_coeffs, preferred_element_type=jnp.float32)
        return coupled, root_part

    coupled, root_part = lax.map(finish_work, (expand_levels, sibling, root_out))
    applied = dense_part + cluster_part + coupled + root_part
    return applied.reshape(leaves * LEAF, W)
```

```python
import jax
import jax.numpy as jnp
from jax import lax
from jax.experimental import pallas as pl
from jax.experimental.pallas import tpu as pltpu
from jax.sharding import PartitionSpec as P

bf16 = jnp.bfloat16
f32 = jnp.float32
contract_first = (((0,), (0,)), ((), ()))
plain = (((1,), (0,)), ((), ()))
in_vmem = pl.BlockSpec(memory_space=pltpu.VMEM)
in_smem = pl.BlockSpec(memory_space=pltpu.SMEM)
in_hbm = pl.BlockSpec(memory_space=pltpu.HBM)
in_place = pl.BlockSpec(memory_space=pl.ANY)
limit = 24 * 1024 * 1024
waited = 10**10


def swapped(x, axis, bit):
    return lax.ppermute(x, axis, [(i, i ^ 1 << bit) for i in range(lax.axis_size(axis))])


def exchanged(x):
    return lax.all_to_all(x, "col", split_axis=0, concat_axis=0, tiled=True)


def ahead(x):
    return pltpu.with_memory_space_constraint(x, pltpu.VMEM)


def left(x):
    return pltpu.with_memory_space_constraint(x, pltpu.HBM)


def mul(a, b, dims=plain):
    return lax.dot_general(a, b, dims, preferred_element_type=f32)


def shape(dims, dtype):
    return jax.ShapeDtypeStruct(dims, dtype)


def call(kernel, out, args, specs=None, out_specs=None, scratch=(), aliases=None, flops=0, name=None):
    return pl.pallas_call(
        kernel,
        out_shape=out,
        in_specs=specs or [in_vmem] * len(args),
        out_specs=out_specs or jax.tree.map(lambda _: in_vmem, out),
        scratch_shapes=scratch,
        input_output_aliases=aliases or {},
        compiler_params=pltpu.CompilerParams(vmem_limit_bytes=limit),
        cost_estimate=pl.CostEstimate(flops=flops, bytes_accessed=flops // 256, transcendentals=0),
        name=name,
    )(*args)


def compress_kernel(
    owner_hbm, x_hbm, compress_hbm, root_hbm,
    low_ref, out_hbm, send_ref, keep_ref,
    owner_ref, x_ref, compress_ref, root_ref, product_ref, out_ref, sems, out_sems,
):
    pieces, size, _ = out_ref.shape
    width = 2 * size
    blocks = pieces // 2
    x_copy = pltpu.make_async_copy(x_hbm, x_ref, sems.at[0])
    owner_copy = pltpu.make_async_copy(owner_hbm, owner_ref, sems.at[1])
    root_copy = pltpu.make_async_copy(root_hbm, root_ref, sems.at[2])
    compress_copies = [
        pltpu.make_async_copy(
            compress_hbm.at[:, b * width : (b + 1) * width],
            compress_ref.at[:, b * width : (b + 1) * width],
            sems.at[3 + b],
        )
        for b in range(blocks)
    ]
    for copy in [x_copy, owner_copy, *compress_copies, root_copy]:
        copy.start()
    x_copy.wait()
    low_ref[...] = x_ref[...].astype(bf16)
    low = low_ref[...]
    owner_copy.wait()
    outs = []
    for b in range(blocks):
        compress_copies[b].wait()
        product = mul(compress_ref[:, b * width : (b + 1) * width], low, contract_first).astype(bf16)
        for k in (2 * b, 2 * b + 1):
            out_ref[k] = product[(k - 2 * b) * size : (k - 2 * b + 1) * size]
            outs.append(
                pltpu.make_async_copy(out_ref.at[k], out_hbm.at[owner_ref[k]], out_sems.at[k])
            )
            outs[-1].start()
    root_copy.wait()
    product_ref[...] = mul(root_ref[...], low, contract_first)
    half = keep_ref.shape[0]
    mine = lax.rem(lax.axis_index("row"), 2)
    keep_ref[...] = product_ref[pl.ds(pl.multiple_of(mine * half, half), half), :]
    send_ref[...] = product_ref[pl.ds(pl.multiple_of((1 - mine) * half, half), half), :].astype(bf16)
    for copy in outs:
        copy.wait()


def compressed(owner_map, x, compress, root_project):
    rows, columns = x.shape
    wide = compress.shape[1]
    pieces = owner_map.shape[0]
    rank = root_project.shape[1]
    outgoing = (pieces, wide // pieces, columns)
    return call(
        compress_kernel,
        [
            shape((rows, columns), bf16),
            shape(outgoing, bf16),
            shape((rank // 2, columns), bf16),
            shape((rank // 2, columns), f32),
        ],
        (left(owner_map), left(x), left(compress), left(root_project)),
        specs=[in_place] * 4,
        out_specs=[in_vmem, in_hbm, in_vmem, in_vmem],
        scratch=[
            pltpu.SMEM(owner_map.shape, jnp.int32),
            pltpu.VMEM((rows, columns), f32),
            pltpu.VMEM((rows, wide), bf16),
            pltpu.VMEM((rows, rank), bf16),
            pltpu.VMEM((rank, columns), f32),
            pltpu.VMEM(outgoing, bf16),
            pltpu.SemaphoreType.DMA((3 + pieces // 2,)),
            pltpu.SemaphoreType.DMA((pieces,)),
        ],
        flops=2 * rows * (wide + rank) * columns,
        name="compress",
    )


def split_kernel(keep_ref, got_ref, low_ref, own_ref, same_ref, other_ref, through_ref, total_ref):
    total_ref[...] = keep_ref[...] + got_ref[...].astype(f32)
    part = own_ref.shape[0]
    mine = lax.rem(lax.axis_index("col"), 2)
    own = total_ref[pl.ds(pl.multiple_of(mine * part, part), part), :]
    own_ref[...] = own
    same_ref[...] = own.astype(bf16)
    other_ref[...] = total_ref[pl.ds(pl.multiple_of((1 - mine) * part, part), part), :].astype(bf16)


def levels_kernel(low_ref, basis_hbm, out_ref, send_ref, basis_ref, sem):
    copy = pltpu.make_async_copy(basis_hbm, basis_ref, sem)
    copy.start()
    low = low_ref[...]
    copy.wait()
    for level in range(basis_ref.shape[0]):
        product = mul(basis_ref[level], low, contract_first)
        out_ref[level] = product
        send_ref[level] = product.astype(bf16)


def middle_kernel(middle_ref, arrived_ref, low_ref, running_ref, own_ref, *refs):
    got, (out_hbm, _, _, out_ref, sems) = refs[:-5], refs[-5:]
    pieces, size, columns = arrived_ref.shape
    total = own_ref[...]
    for got_ref in got:
        total += got_ref[...].astype(f32)
    part = total.astype(bf16)
    arrived = arrived_ref[...].reshape(pieces * size, columns)
    copies = []
    for b in range(0, pieces, 2):
        product = mul(middle_ref[b * size : (b + 2) * size, :], arrived).astype(bf16)
        for k in (b, b + 1):
            out_ref[k, :size] = product[(k - b) * size : (k - b + 1) * size]
            out_ref[k, size:] = part
            copies.append(pltpu.make_async_copy(out_ref.at[k], out_hbm.at[k], sems.at[k]))
            copies[-1].start()
    for copy in copies:
        copy.wait()


def add_kernel(keep_ref, got_ref, sum_ref, send_ref):
    total = keep_ref[...] + got_ref[...].astype(f32)
    sum_ref[...] = total
    send_ref[...] = total.astype(bf16)


def dense_kernel(
    owner_hbm, low_ref, inverse_hbm, row_hbm, expand_hbm, root_hbm,
    out_ref, row_ref, expand_ref, root_ref,
    owner_ref, inverse_ref, sems, expand_sems,
):
    owner_copy = pltpu.make_async_copy(owner_hbm, owner_ref, sems.at[0])
    inverse_copy = pltpu.make_async_copy(inverse_hbm, inverse_ref, sems.at[1])
    row_copy = pltpu.make_async_copy(row_hbm, row_ref, sems.at[2])
    root_copy = pltpu.make_async_copy(root_hbm, root_ref, sems.at[3])
    for copy in (owner_copy, inverse_copy, row_copy, root_copy):
        copy.start()
    owner_copy.wait()
    pieces = expand_sems.shape[0]
    size = expand_ref.shape[1] // pieces
    expand_copies = []
    for k in range(pieces):
        place = pl.ds(pl.multiple_of(owner_ref[k] * size, size), size)
        expand_copies.append(
            pltpu.make_async_copy(
                expand_hbm.at[:, k * size : (k + 1) * size], expand_ref.at[:, place], expand_sems.at[k]
            )
        )
        expand_copies[-1].start()
    inverse_copy.wait()
    out_ref[...] = mul(inverse_ref[...], low_ref[...])
    for copy in (row_copy, root_copy, *expand_copies):
        copy.wait()


def couple_kernel(dense_ref, expand_ref, *refs):
    out_ref = refs[-1]
    total = dense_ref[...]
    for level, sibling_ref in enumerate(refs[:-1]):
        total += mul(expand_ref[level], sibling_ref[...])
    out_ref[...] = total


def root_kernel(returned_ref, partial_ref, out_ref, through_ref):
    part = out_ref.shape[0] // 2
    size = returned_ref.shape[1] - part
    for parity in range(2):
        total = jnp.zeros((part, out_ref.shape[1]), f32)
        for d in range(parity, returned_ref.shape[0], 2):
            total += returned_ref[d, size:, :].astype(f32)
        out_ref[parity * part : (parity + 1) * part] = total.astype(bf16)


def expand_kernel(partial_ref, expand_ref, returned_ref, out_ref):
    pieces = returned_ref.shape[0]
    size = expand_ref.shape[1] // pieces
    returned = jnp.concatenate([returned_ref[k, :size] for k in range(pieces)], axis=0)
    out_ref[...] = partial_ref[...] + mul(expand_ref[...], returned)


def final_kernel(partial_ref, root_expand_ref, mine_ref, other_ref, out_ref, root_ref):
    half = mine_ref.shape[0]
    mine = lax.rem(lax.axis_index("row"), 2)
    root_ref[pl.ds(pl.multiple_of(mine * half, half), half), :] = mine_ref[...]
    root_ref[pl.ds(pl.multiple_of((1 - mine) * half, half), half), :] = other_ref[...]
    out_ref[...] = partial_ref[...] + mul(root_expand_ref[...], root_ref[...])


def per_device(
    right_side,
    leaf_inverse,
    compress,
    middle,
    expand,
    row_project,
    row_expand,
    root_project,
    root_expand,
    owner_map,
):
    rows, columns = right_side.shape
    levels, _, rank = row_project.shape
    row_count = lax.axis_size("row")
    col_count = lax.axis_size("col")
    half = rank // 2
    part = half // 2

    low, outgoing, send, keep = compressed(owner_map, right_side, compress, root_project)
    got = swapped(send, "row", 0)
    arrived = exchanged(outgoing)
    own, same, other, low = call(
        split_kernel,
        [
            shape((part, columns), f32),
            shape((part, columns), bf16),
            shape((part, columns), bf16),
            shape(low.shape, bf16),
        ],
        (keep, got, low),
        scratch=[pltpu.VMEM((half, columns), f32)],
        aliases={2: 3},
        flops=waited,
        name="root_split",
    )
    parts = []
    for row_step in range(0, row_count, 2):
        for col_step in range(2):
            if row_step or col_step:
                pairs = [
                    (r * col_count + c, (r ^ row_step) * col_count + (c ^ col_step))
                    for r in range(row_count)
                    for c in range(col_count)
                ]
                parts.append(lax.ppermute(other if col_step else same, ("row", "col"), pairs))
    running, level_send = call(
        levels_kernel,
        [shape((levels, rank, columns), f32), shape((levels, rank, columns), bf16)],
        (low, left(row_project)),
        specs=[in_vmem, in_place],
        scratch=[pltpu.VMEM(row_project.shape, bf16), pltpu.SemaphoreType.DMA],
        flops=2 * rows * rank * levels * columns,
        name="levels",
    )
    partner = swapped(level_send, "row", 0)

    size = middle.shape[0] // col_count
    mixed_shape = (col_count, size + part, columns)
    mixed, low, running = call(
        middle_kernel,
        [shape(mixed_shape, bf16), shape(low.shape, bf16), shape(running.shape, f32)],
        (ahead(middle), arrived, low, running, own, *parts),
        out_specs=[in_hbm, in_vmem, in_vmem],
        scratch=[pltpu.VMEM(mixed_shape, bf16), pltpu.SemaphoreType.DMA((col_count,))],
        aliases={2: 1, 3: 2},
        flops=2 * middle.shape[0] * middle.shape[1] * columns,
        name="middle",
    )
    returned = exchanged(mixed)

    dense, row_expand, expand, root_expand = call(
        dense_kernel,
        [
            shape((rows, columns), f32),
            pltpu.VMEM(row_expand.shape, bf16),
            pltpu.VMEM(expand.shape, bf16),
            pltpu.VMEM(root_expand.shape, bf16),
        ],
        (left(owner_map), low, left(leaf_inverse), left(row_expand), left(expand), left(root_expand)),
        specs=[in_place, in_vmem] + [in_place] * 4,
        scratch=[
            pltpu.SMEM(owner_map.shape, jnp.int32),
            pltpu.VMEM(leaf_inverse.shape, bf16),
            pltpu.SemaphoreType.DMA((4,)),
            pltpu.SemaphoreType.DMA((col_count,)),
        ],
        flops=2 * rows * rows * columns,
        name="dense",
    )
    siblings = [partner[0]]
    for bit in range(1, levels):
        running, level_send = call(
            add_kernel,
            [shape(running[1:].shape, f32), shape(running[1:].shape, bf16)],
            (running[1:], partner[1:]),
            name="level_sum",
        )
        partner = swapped(level_send, "row", bit)
        siblings.append(partner[0])
    partial = call(
        couple_kernel,
        shape((rows, columns), f32),
        (dense, row_expand, *siblings),
        flops=2 * rows * rank * levels * columns,
        name="couple",
    )

    root_mine, partial = call(
        root_kernel,
        [shape((half, columns), bf16), shape(partial.shape, f32)],
        (returned, partial),
        aliases={1: 1},
        name="root_sum",
    )
    root_other = swapped(root_mine, "row", 0)
    partial = call(
        expand_kernel,
        shape((rows, columns), f32),
        (partial, expand, returned),
        flops=2 * rows * expand.shape[1] * columns,
        name="expand",
    )
    return call(
        final_kernel,
        shape((rows, columns), f32),
        (partial, root_expand, root_mine, root_other),
        scratch=[pltpu.VMEM((rank, columns), bf16)],
        flops=2 * rows * rank * columns,
        name="final",
    )


def solution(mesh):
    leaves = P(("row", "col"), None)
    levels = P(None, ("row", "col"), None)
    return jax.shard_map(
        per_device,
        mesh=mesh,
        in_specs=(leaves,) * 5 + (levels,) * 2 + (leaves,) * 2 + (P(),),
        out_specs=leaves,
        check_vma=False,
    )
```

```python
import jax
import jax.numpy as jnp
from jax import lax
from jax.experimental import pallas as pl
from jax.experimental.pallas import tpu as pltpu
from jax.sharding import PartitionSpec as P

bf16 = jnp.bfloat16
f32 = jnp.float32
contract_first = (((0,), (0,)), ((), ()))
plain = (((1,), (0,)), ((), ()))
in_vmem = pl.BlockSpec(memory_space=pltpu.VMEM)
in_smem = pl.BlockSpec(memory_space=pltpu.SMEM)
in_hbm = pl.BlockSpec(memory_space=pltpu.HBM)
in_place = pl.BlockSpec(memory_space=pl.ANY)
limit = 24 * 1024 * 1024
waited = 10**10


def swapped(x, axis, bit):
    return lax.ppermute(x, axis, [(i, i ^ 1 << bit) for i in range(lax.axis_size(axis))])


def slots(count):
    block = count // 4
    return [quarter * block + i for quarter in (2, 0, 1, 3) for i in range(block)]


def slot_of(device, count):
    block = count // 4
    quarter = device // block
    moved = jnp.where(quarter == 3, 3, jnp.where(quarter == 2, 0, quarter + 1))
    return device + (moved - quarter) * block


def exchanged(x):
    groups = [slots(lax.axis_size("col"))]
    return lax.all_to_all(x, "col", 0, 0, tiled=True, axis_index_groups=groups)


def ahead(x):
    return pltpu.with_memory_space_constraint(x, pltpu.VMEM)


def left(x):
    return pltpu.with_memory_space_constraint(x, pltpu.HBM)


def mul(a, b, dims=plain):
    return lax.dot_general(a, b, dims, preferred_element_type=f32)


def shape(dims, dtype):
    return jax.ShapeDtypeStruct(dims, dtype)


def call(kernel, out, args, specs=None, out_specs=None, scratch=(), aliases=None, flops=0, name=None):
    return pl.pallas_call(
        kernel,
        out_shape=out,
        in_specs=specs or [in_vmem] * len(args),
        out_specs=out_specs or jax.tree.map(lambda _: in_vmem, out),
        scratch_shapes=scratch,
        input_output_aliases=aliases or {},
        compiler_params=pltpu.CompilerParams(vmem_limit_bytes=limit),
        cost_estimate=pl.CostEstimate(flops=flops, bytes_accessed=flops // 256, transcendentals=0),
        name=name,
    )(*args)


def compress_kernel(
    owner_hbm, x_hbm, compress_hbm, root_hbm,
    low_ref, out_hbm, send_ref, keep_ref,
    owner_ref, x_ref, compress_ref, root_ref, product_ref, out_ref, sems, compress_sems, out_sems,
):
    pieces, size, _ = out_ref.shape
    blocks = compress_sems.shape[0]
    count = pieces // blocks
    width = count * size
    x_copy = pltpu.make_async_copy(x_hbm, x_ref, sems.at[0])
    owner_copy = pltpu.make_async_copy(owner_hbm, owner_ref, sems.at[1])
    root_copy = pltpu.make_async_copy(root_hbm, root_ref, sems.at[2])
    compress_copies = [
        pltpu.make_async_copy(
            compress_hbm.at[:, b * width : (b + 1) * width],
            compress_ref.at[:, b * width : (b + 1) * width],
            compress_sems.at[b],
        )
        for b in range(blocks)
    ]
    for copy in [x_copy, owner_copy, *compress_copies, root_copy]:
        copy.start()
    x_copy.wait()
    low_ref[...] = x_ref[...].astype(bf16)
    low = low_ref[...]
    flat = low.T
    owner_copy.wait()
    outs = []
    for b in range(blocks):
        compress_copies[b].wait()
        product = mul(flat, compress_ref[:, b * width : (b + 1) * width]).astype(bf16).T
        out_ref[b * count : (b + 1) * count] = product.reshape(count, size, -1)
        for k in range(b * count, (b + 1) * count):
            outs.append(
                pltpu.make_async_copy(out_ref.at[k], out_hbm.at[slot_of(owner_ref[k], pieces)], out_sems.at[k])
            )
            outs[-1].start()
    root_copy.wait()
    product_ref[...] = mul(root_ref[...], low, contract_first)
    half = keep_ref.shape[0]
    mine = lax.rem(lax.axis_index("row"), 2)
    keep_ref[...] = product_ref[pl.ds(pl.multiple_of(mine * half, half), half), :]
    send_ref[...] = product_ref[pl.ds(pl.multiple_of((1 - mine) * half, half), half), :].astype(bf16)
    for copy in outs:
        copy.wait()


def compressed(owner_map, x, compress, root_project):
    rows, columns = x.shape
    wide = compress.shape[1]
    pieces = owner_map.shape[0]
    rank = root_project.shape[1]
    outgoing = (pieces, wide // pieces, columns)
    return call(
        compress_kernel,
        [
            shape((rows, columns), bf16),
            shape(outgoing, bf16),
            shape((rank // 2, columns), bf16),
            shape((rank // 2, columns), f32),
        ],
        (left(owner_map), left(x), left(compress), left(root_project)),
        specs=[in_place] * 4,
        out_specs=[in_vmem, in_hbm, in_vmem, in_vmem],
        scratch=[
            pltpu.SMEM(owner_map.shape, jnp.int32),
            pltpu.VMEM((rows, columns), f32),
            pltpu.VMEM((rows, wide), bf16),
            pltpu.VMEM((rows, rank), bf16),
            pltpu.VMEM((rank, columns), f32),
            pltpu.VMEM(outgoing, bf16),
            pltpu.SemaphoreType.DMA((3,)),
            pltpu.SemaphoreType.DMA((2,)),
            pltpu.SemaphoreType.DMA((pieces,)),
        ],
        flops=2 * rows * (wide + rank) * columns,
        name="compress",
    )


def split_kernel(keep_ref, got_ref, low_ref, own_ref, same_ref, other_ref, through_ref, total_ref):
    total_ref[...] = keep_ref[...] + got_ref[...].astype(f32)
    part = own_ref.shape[0]
    mine = lax.rem(lax.axis_index("col"), 2)
    own = total_ref[pl.ds(pl.multiple_of(mine * part, part), part), :]
    own_ref[...] = own
    same_ref[...] = own.astype(bf16)
    other_ref[...] = total_ref[pl.ds(pl.multiple_of((1 - mine) * part, part), part), :].astype(bf16)


def levels_kernel(low_ref, basis_hbm, out_ref, send_ref, basis_ref, sem):
    copy = pltpu.make_async_copy(basis_hbm, basis_ref, sem)
    copy.start()
    low = low_ref[...]
    copy.wait()
    for level in range(basis_ref.shape[0]):
        product = mul(basis_ref[level], low, contract_first)
        out_ref[level] = product
        send_ref[level] = product.astype(bf16)


def middle_kernel(middle_ref, arrived_ref, low_ref, running_ref, own_ref, *refs):
    got, (out_hbm, _, _, out_ref, sems) = refs[:-5], refs[-5:]
    pieces, size, columns = arrived_ref.shape
    total = own_ref[...]
    for got_ref in got:
        total += got_ref[...].astype(f32)
    part = total.astype(bf16)
    order = slots(pieces)
    arrived = jnp.concatenate([arrived_ref[order.index(c)] for c in range(pieces)], axis=0)
    copies = []
    for k in range(pieces):
        out_ref[k, :size] = mul(middle_ref[k * size : (k + 1) * size, :], arrived).astype(bf16)
        out_ref[k, size:] = part
        copies.append(pltpu.make_async_copy(out_ref.at[k], out_hbm.at[order.index(k)], sems.at[k]))
        copies[-1].start()
    for copy in copies:
        copy.wait()


def add_kernel(keep_ref, got_ref, sum_ref, send_ref):
    total = keep_ref[...] + got_ref[...].astype(f32)
    sum_ref[...] = total
    send_ref[...] = total.astype(bf16)


def dense_kernel(
    owner_hbm, low_ref, inverse_hbm, row_hbm, expand_hbm, root_hbm,
    out_ref, row_ref, expand_ref, root_ref,
    owner_ref, inverse_ref, sems, expand_sems,
):
    owner_copy = pltpu.make_async_copy(owner_hbm, owner_ref, sems.at[0])
    inverse_copy = pltpu.make_async_copy(inverse_hbm, inverse_ref, sems.at[1])
    row_copy = pltpu.make_async_copy(row_hbm, row_ref, sems.at[2])
    root_copy = pltpu.make_async_copy(root_hbm, root_ref, sems.at[3])
    for copy in (owner_copy, inverse_copy, row_copy, root_copy):
        copy.start()
    owner_copy.wait()
    pieces = expand_sems.shape[0]
    size = expand_ref.shape[1] // pieces
    expand_copies = []
    for k in range(pieces):
        place = pl.ds(pl.multiple_of(slot_of(owner_ref[k], pieces) * size, size), size)
        expand_copies.append(
            pltpu.make_async_copy(
                expand_hbm.at[:, k * size : (k + 1) * size], expand_ref.at[:, place], expand_sems.at[k]
            )
        )
        expand_copies[-1].start()
    inverse_copy.wait()
    out_ref[...] = mul(inverse_ref[...], low_ref[...])
    for copy in (row_copy, root_copy, *expand_copies):
        copy.wait()


def couple_kernel(dense_ref, expand_ref, *refs):
    out_ref = refs[-1]
    total = dense_ref[...]
    for level, sibling_ref in enumerate(refs[:-1]):
        total += mul(expand_ref[level], sibling_ref[...])
    out_ref[...] = total


def root_kernel(returned_ref, partial_ref, out_ref, through_ref):
    part = out_ref.shape[0] // 2
    size = returned_ref.shape[1] - part
    order = slots(returned_ref.shape[0])
    for parity in range(2):
        total = jnp.zeros((part, out_ref.shape[1]), f32)
        for k in range(returned_ref.shape[0]):
            if order[k] % 2 == parity:
                total += returned_ref[k, size:, :].astype(f32)
        out_ref[parity * part : (parity + 1) * part] = total.astype(bf16)


def expand_kernel(partial_ref, expand_ref, returned_ref, out_ref):
    pieces = returned_ref.shape[0]
    size = expand_ref.shape[1] // pieces
    returned = jnp.concatenate([returned_ref[k, :size] for k in range(pieces)], axis=0)
    out_ref[...] = partial_ref[...] + mul(expand_ref[...], returned)


def final_kernel(partial_ref, root_expand_ref, mine_ref, other_ref, out_ref, root_ref):
    half = mine_ref.shape[0]
    mine = lax.rem(lax.axis_index("row"), 2)
    root_ref[pl.ds(pl.multiple_of(mine * half, half), half), :] = mine_ref[...]
    root_ref[pl.ds(pl.multiple_of((1 - mine) * half, half), half), :] = other_ref[...]
    out_ref[...] = partial_ref[...] + mul(root_expand_ref[...], root_ref[...])


def per_device(
    right_side,
    leaf_inverse,
    compress,
    middle,
    expand,
    row_project,
    row_expand,
    root_project,
    root_expand,
    owner_map,
):
    rows, columns = right_side.shape
    levels, _, rank = row_project.shape
    row_count = lax.axis_size("row")
    col_count = lax.axis_size("col")
    half = rank // 2
    part = half // 2

    low, outgoing, send, keep = compressed(owner_map, right_side, compress, root_project)
    got = swapped(send, "row", 0)
    arrived = exchanged(outgoing)
    own, same, other, low = call(
        split_kernel,
        [
            shape((part, columns), f32),
            shape((part, columns), bf16),
            shape((part, columns), bf16),
            shape(low.shape, bf16),
        ],
        (keep, got, low),
        scratch=[pltpu.VMEM((half, columns), f32)],
        aliases={2: 3},
        flops=waited,
        name="root_split",
    )
    parts = []
    for row_step in range(0, row_count, 2):
        for col_step in range(2):
            if row_step or col_step:
                pairs = [
                    (r * col_count + c, (r ^ row_step) * col_count + (c ^ col_step))
                    for r in range(row_count)
                    for c in range(col_count)
                ]
                parts.append(lax.ppermute(other if col_step else same, ("row", "col"), pairs))
    running, level_send = call(
        levels_kernel,
        [shape((levels, rank, columns), f32), shape((levels, rank, columns), bf16)],
        (low, left(row_project)),
        specs=[in_vmem, in_place],
        scratch=[pltpu.VMEM(row_project.shape, bf16), pltpu.SemaphoreType.DMA],
        flops=2 * rows * rank * levels * columns,
        name="levels",
    )
    partner = swapped(level_send, "row", 0)

    size = middle.shape[0] // col_count
    mixed_shape = (col_count, size + part, columns)
    mixed, low, running = call(
        middle_kernel,
        [shape(mixed_shape, bf16), shape(low.shape, bf16), shape(running.shape, f32)],
        (ahead(middle), arrived, low, running, own, *parts),
        out_specs=[in_hbm, in_vmem, in_vmem],
        scratch=[pltpu.VMEM(mixed_shape, bf16), pltpu.SemaphoreType.DMA((col_count,))],
        aliases={2: 1, 3: 2},
        flops=2 * middle.shape[0] * middle.shape[1] * columns,
        name="middle",
    )
    returned = exchanged(mixed)

    dense, row_expand, expand, root_expand = call(
        dense_kernel,
        [
            shape((rows, columns), f32),
            pltpu.VMEM(row_expand.shape, bf16),
            pltpu.VMEM(expand.shape, bf16),
            pltpu.VMEM(root_expand.shape, bf16),
        ],
        (left(owner_map), low, left(leaf_inverse), left(row_expand), left(expand), left(root_expand)),
        specs=[in_place, in_vmem] + [in_place] * 4,
        scratch=[
            pltpu.SMEM(owner_map.shape, jnp.int32),
            pltpu.VMEM(leaf_inverse.shape, bf16),
            pltpu.SemaphoreType.DMA((4,)),
            pltpu.SemaphoreType.DMA((col_count,)),
        ],
        flops=2 * rows * rows * columns,
        name="dense",
    )
    siblings = [partner[0]]
    for bit in range(1, levels):
        running, level_send = call(
            add_kernel,
            [shape(running[1:].shape, f32), shape(running[1:].shape, bf16)],
            (running[1:], partner[1:]),
            name="level_sum",
        )
        partner = swapped(level_send, "row", bit)
        siblings.append(partner[0])
    partial = call(
        couple_kernel,
        shape((rows, columns), f32),
        (dense, row_expand, *siblings),
        flops=2 * rows * rank * levels * columns,
        name="couple",
    )

    root_mine, partial = call(
        root_kernel,
        [shape((half, columns), bf16), shape(partial.shape, f32)],
        (returned, partial),
        aliases={1: 1},
        name="root_sum",
    )
    root_other = swapped(root_mine, "row", 0)
    partial = call(
        expand_kernel,
        shape((rows, columns), f32),
        (partial, expand, returned),
        flops=2 * rows * expand.shape[1] * columns,
        name="expand",
    )
    return call(
        final_kernel,
        shape((rows, columns), f32),
        (partial, root_expand, root_mine, root_other),
        scratch=[pltpu.VMEM((rank, columns), bf16)],
        flops=2 * rows * rank * columns,
        name="final",
    )


def solution(mesh):
    leaves = P(("row", "col"), None)
    levels = P(None, ("row", "col"), None)
    return jax.shard_map(
        per_device,
        mesh=mesh,
        in_specs=(leaves,) * 5 + (levels,) * 2 + (leaves,) * 2 + (P(),),
        out_specs=leaves,
        check_vma=False,
    )
```

```python
import jax
import jax.numpy as jnp
from jax import lax
from jax.experimental import pallas as pl
from jax.experimental.pallas import tpu as pltpu
from jax.sharding import PartitionSpec as P

bf16 = jnp.bfloat16
f32 = jnp.float32
contract_first = (((0,), (0,)), ((), ()))
plain = (((1,), (0,)), ((), ()))
in_vmem = pl.BlockSpec(memory_space=pltpu.VMEM)
in_smem = pl.BlockSpec(memory_space=pltpu.SMEM)
in_hbm = pl.BlockSpec(memory_space=pltpu.HBM)
in_place = pl.BlockSpec(memory_space=pl.ANY)
limit = 24 * 1024 * 1024
waited = 10**10


def swapped(x, axis, bit):
    return lax.ppermute(x, axis, [(i, i ^ 1 << bit) for i in range(lax.axis_size(axis))])


out_order = (4, 2, 0, 6, 5, 3, 1, 7)
back_order = (4, 2, 0, 6, 5, 3, 1, 7)


def slots(order, count):
    parts = len(order)
    if count % parts:
        return list(range(count))
    block = count // parts
    return [part * block + i for part in order for i in range(block)]


def slot_of(order, device, count):
    return sum(jnp.where(device == d, i, 0) for i, d in enumerate(slots(order, count)))


def exchanged(x, order):
    groups = [slots(order, lax.axis_size("col"))]
    return lax.all_to_all(x, "col", 0, 0, tiled=True, axis_index_groups=groups)


def ahead(x):
    return pltpu.with_memory_space_constraint(x, pltpu.VMEM)


def left(x):
    return pltpu.with_memory_space_constraint(x, pltpu.HBM)


def mul(a, b, dims=plain):
    return lax.dot_general(a, b, dims, preferred_element_type=f32)


def shape(dims, dtype):
    return jax.ShapeDtypeStruct(dims, dtype)


def call(kernel, out, args, specs=None, out_specs=None, scratch=(), aliases=None, flops=0, name=None):
    return pl.pallas_call(
        kernel,
        out_shape=out,
        in_specs=specs or [in_vmem] * len(args),
        out_specs=out_specs or jax.tree.map(lambda _: in_vmem, out),
        scratch_shapes=scratch,
        input_output_aliases=aliases or {},
        compiler_params=pltpu.CompilerParams(vmem_limit_bytes=limit),
        cost_estimate=pl.CostEstimate(flops=flops, bytes_accessed=flops // 256, transcendentals=0),
        name=name,
    )(*args)


def compress_kernel(
    owner_hbm, x_hbm, compress_hbm, root_hbm,
    low_ref, out_hbm, send_ref, keep_ref,
    owner_ref, x_ref, compress_ref, root_ref, product_ref, out_ref, sems, compress_sems, out_sems,
):
    pieces, size, _ = out_ref.shape
    blocks = compress_sems.shape[0]
    count = pieces // blocks
    width = count * size
    x_copy = pltpu.make_async_copy(x_hbm, x_ref, sems.at[0])
    owner_copy = pltpu.make_async_copy(owner_hbm, owner_ref, sems.at[1])
    root_copy = pltpu.make_async_copy(root_hbm, root_ref, sems.at[2])
    compress_copies = [
        pltpu.make_async_copy(
            compress_hbm.at[:, b * width : (b + 1) * width],
            compress_ref.at[:, b * width : (b + 1) * width],
            compress_sems.at[b],
        )
        for b in range(blocks)
    ]
    for copy in [x_copy, owner_copy, *compress_copies, root_copy]:
        copy.start()
    x_copy.wait()
    low_ref[...] = x_ref[...].astype(bf16)
    low = low_ref[...]
    flat = low.T
    owner_copy.wait()
    outs = []
    for b in range(blocks):
        compress_copies[b].wait()
        product = mul(flat, compress_ref[:, b * width : (b + 1) * width]).astype(bf16).T
        out_ref[b * count : (b + 1) * count] = product.reshape(count, size, -1)
        for k in range(b * count, (b + 1) * count):
            outs.append(
                pltpu.make_async_copy(out_ref.at[k], out_hbm.at[slot_of(out_order, owner_ref[k], pieces)], out_sems.at[k])
            )
            outs[-1].start()
    root_copy.wait()
    product_ref[...] = mul(root_ref[...], low, contract_first)
    half = keep_ref.shape[0]
    mine = lax.rem(lax.axis_index("row"), 2)
    keep_ref[...] = product_ref[pl.ds(pl.multiple_of(mine * half, half), half), :]
    send_ref[...] = product_ref[pl.ds(pl.multiple_of((1 - mine) * half, half), half), :].astype(bf16)
    for copy in outs:
        copy.wait()


def compressed(owner_map, x, compress, root_project):
    rows, columns = x.shape
    wide = compress.shape[1]
    pieces = owner_map.shape[0]
    rank = root_project.shape[1]
    outgoing = (pieces, wide // pieces, columns)
    return call(
        compress_kernel,
        [
            shape((rows, columns), bf16),
            shape(outgoing, bf16),
            shape((rank // 2, columns), bf16),
            shape((rank // 2, columns), f32),
        ],
        (left(owner_map), left(x), left(compress), left(root_project)),
        specs=[in_place] * 4,
        out_specs=[in_vmem, in_hbm, in_vmem, in_vmem],
        scratch=[
            pltpu.SMEM(owner_map.shape, jnp.int32),
            pltpu.VMEM((rows, columns), f32),
            pltpu.VMEM((rows, wide), bf16),
            pltpu.VMEM((rows, rank), bf16),
            pltpu.VMEM((rank, columns), f32),
            pltpu.VMEM(outgoing, bf16),
            pltpu.SemaphoreType.DMA((3,)),
            pltpu.SemaphoreType.DMA((2,)),
            pltpu.SemaphoreType.DMA((pieces,)),
        ],
        flops=2 * rows * (wide + rank) * columns,
        name="compress",
    )


def split_kernel(keep_ref, got_ref, low_ref, own_ref, same_ref, other_ref, through_ref, total_ref):
    total_ref[...] = keep_ref[...] + got_ref[...].astype(f32)
    part = own_ref.shape[0]
    mine = lax.rem(lax.axis_index("col"), 2)
    own = total_ref[pl.ds(pl.multiple_of(mine * part, part), part), :]
    own_ref[...] = own
    same_ref[...] = own.astype(bf16)
    other_ref[...] = total_ref[pl.ds(pl.multiple_of((1 - mine) * part, part), part), :].astype(bf16)


def levels_kernel(low_ref, basis_hbm, out_ref, send_ref, basis_ref, sem):
    copy = pltpu.make_async_copy(basis_hbm, basis_ref, sem)
    copy.start()
    low = low_ref[...]
    copy.wait()
    for level in range(basis_ref.shape[0]):
        product = mul(basis_ref[level], low, contract_first)
        out_ref[level] = product
        send_ref[level] = product.astype(bf16)


def middle_kernel(middle_ref, arrived_ref, low_ref, running_ref, own_ref, *refs):
    got, (out_hbm, _, _, out_ref, sems) = refs[:-5], refs[-5:]
    pieces, size, columns = arrived_ref.shape
    total = own_ref[...]
    for got_ref in got:
        total += got_ref[...].astype(f32)
    part = total.astype(bf16)
    order = slots(out_order, pieces)
    back = slots(back_order, pieces)
    arrived = jnp.concatenate([arrived_ref[order.index(c)] for c in range(pieces)], axis=0)
    copies = []
    for k in range(pieces):
        out_ref[k, :size] = mul(middle_ref[k * size : (k + 1) * size, :], arrived).astype(bf16)
        out_ref[k, size:] = part
        copies.append(pltpu.make_async_copy(out_ref.at[k], out_hbm.at[back.index(k)], sems.at[k]))
        copies[-1].start()
    for copy in copies:
        copy.wait()


def add_kernel(keep_ref, got_ref, send_ref, *sum_ref):
    total = keep_ref[1:] + got_ref[1:].astype(f32)
    send_ref[...] = total.astype(bf16)
    if sum_ref:
        sum_ref[0][...] = total


def dense_kernel(
    owner_hbm, low_ref, inverse_hbm, row_hbm, expand_hbm, root_hbm,
    out_ref, row_ref, expand_ref, root_ref,
    owner_ref, inverse_ref, sems, expand_sems,
):
    owner_copy = pltpu.make_async_copy(owner_hbm, owner_ref, sems.at[0])
    inverse_copy = pltpu.make_async_copy(inverse_hbm, inverse_ref, sems.at[1])
    row_copy = pltpu.make_async_copy(row_hbm, row_ref, sems.at[2])
    root_copy = pltpu.make_async_copy(root_hbm, root_ref, sems.at[3])
    for copy in (owner_copy, inverse_copy, row_copy, root_copy):
        copy.start()
    owner_copy.wait()
    pieces = expand_sems.shape[0]
    size = expand_ref.shape[1] // pieces
    expand_copies = []
    for k in range(pieces):
        place = pl.ds(pl.multiple_of(slot_of(back_order, owner_ref[k], pieces) * size, size), size)
        expand_copies.append(
            pltpu.make_async_copy(
                expand_hbm.at[:, k * size : (k + 1) * size], expand_ref.at[:, place], expand_sems.at[k]
            )
        )
        expand_copies[-1].start()
    inverse_copy.wait()
    out_ref[...] = mul(inverse_ref[...], low_ref[...])
    for copy in (row_copy, root_copy, *expand_copies):
        copy.wait()


def couple_kernel(dense_ref, expand_ref, *refs):
    out_ref = refs[-1]
    total = dense_ref[...]
    for level, sibling_ref in enumerate(refs[:-1]):
        total += mul(expand_ref[level], sibling_ref[0])
    out_ref[...] = total


def root_kernel(returned_ref, partial_ref, out_ref, through_ref):
    part = out_ref.shape[0] // 2
    size = returned_ref.shape[1] - part
    order = slots(back_order, returned_ref.shape[0])
    for parity in range(2):
        total = jnp.zeros((part, out_ref.shape[1]), f32)
        for k in range(returned_ref.shape[0]):
            if order[k] % 2 == parity:
                total += returned_ref[k, size:, :].astype(f32)
        out_ref[parity * part : (parity + 1) * part] = total.astype(bf16)


def expand_kernel(partial_ref, expand_ref, returned_ref, out_ref):
    pieces = returned_ref.shape[0]
    size = expand_ref.shape[1] // pieces
    returned = jnp.concatenate([returned_ref[k, :size] for k in range(pieces)], axis=0)
    out_ref[...] = partial_ref[...] + mul(expand_ref[...], returned)


def final_kernel(partial_ref, root_expand_ref, mine_ref, other_ref, out_ref, root_ref):
    half = mine_ref.shape[0]
    mine = lax.rem(lax.axis_index("row"), 2)
    root_ref[pl.ds(pl.multiple_of(mine * half, half), half), :] = mine_ref[...]
    root_ref[pl.ds(pl.multiple_of((1 - mine) * half, half), half), :] = other_ref[...]
    out_ref[...] = partial_ref[...] + mul(root_expand_ref[...], root_ref[...])


def per_device(
    right_side,
    leaf_inverse,
    compress,
    middle,
    expand,
    row_project,
    row_expand,
    root_project,
    root_expand,
    owner_map,
):
    rows, columns = right_side.shape
    levels, _, rank = row_project.shape
    row_count = lax.axis_size("row")
    col_count = lax.axis_size("col")
    half = rank // 2
    part = half // 2

    low, outgoing, send, keep = compressed(owner_map, right_side, compress, root_project)
    got = swapped(send, "row", 0)
    arrived = exchanged(outgoing, out_order)
    own, same, other, low = call(
        split_kernel,
        [
            shape((part, columns), f32),
            shape((part, columns), bf16),
            shape((part, columns), bf16),
            shape(low.shape, bf16),
        ],
        (keep, got, low),
        scratch=[pltpu.VMEM((half, columns), f32)],
        aliases={2: 3},
        flops=waited,
        name="root_split",
    )
    parts = []
    for row_step in range(0, row_count, 2):
        for col_step in range(2):
            if row_step or col_step:
                pairs = [
                    (r * col_count + c, (r ^ row_step) * col_count + (c ^ col_step))
                    for r in range(row_count)
                    for c in range(col_count)
                ]
                parts.append(lax.ppermute(other if col_step else same, ("row", "col"), pairs))
    running, level_send = call(
        levels_kernel,
        [shape((levels, rank, columns), f32), shape((levels, rank, columns), bf16)],
        (low, left(row_project)),
        specs=[in_vmem, in_place],
        scratch=[pltpu.VMEM(row_project.shape, bf16), pltpu.SemaphoreType.DMA],
        flops=2 * rows * rank * levels * columns,
        name="levels",
    )
    partner = swapped(level_send, "row", 0)

    size = middle.shape[0] // col_count
    mixed_shape = (col_count, size + part, columns)
    mixed, low, running = call(
        middle_kernel,
        [shape(mixed_shape, bf16), shape(low.shape, bf16), shape(running.shape, f32)],
        (ahead(middle), arrived, low, running, own, *parts),
        out_specs=[in_hbm, in_vmem, in_vmem],
        scratch=[pltpu.VMEM(mixed_shape, bf16), pltpu.SemaphoreType.DMA((col_count,))],
        aliases={2: 1, 3: 2},
        flops=2 * middle.shape[0] * middle.shape[1] * columns,
        name="middle",
    )
    returned = exchanged(mixed, back_order)

    dense, row_expand, expand, root_expand = call(
        dense_kernel,
        [
            shape((rows, columns), f32),
            pltpu.VMEM(row_expand.shape, bf16),
            pltpu.VMEM(expand.shape, bf16),
            pltpu.VMEM(root_expand.shape, bf16),
        ],
        (left(owner_map), low, left(leaf_inverse), left(row_expand), left(expand), left(root_expand)),
        specs=[in_place, in_vmem] + [in_place] * 4,
        scratch=[
            pltpu.SMEM(owner_map.shape, jnp.int32),
            pltpu.VMEM(leaf_inverse.shape, bf16),
            pltpu.SemaphoreType.DMA((4,)),
            pltpu.SemaphoreType.DMA((col_count,)),
        ],
        flops=2 * rows * rows * columns,
        name="dense",
    )
    siblings = [partner]
    for bit in range(1, levels):
        dims = (levels - bit, rank, columns)
        out = [shape(dims, bf16)] + [shape(dims, f32)] * (bit + 1 < levels)
        level_send, *running = call(add_kernel, out, (running, partner), name="level_sum")
        running = running[0] if running else None
        partner = swapped(level_send, "row", bit)
        siblings.append(partner)
    partial = call(
        couple_kernel,
        shape((rows, columns), f32),
        (dense, row_expand, *siblings),
        flops=2 * rows * rank * levels * columns,
        name="couple",
    )

    root_mine, partial = call(
        root_kernel,
        [shape((half, columns), bf16), shape(partial.shape, f32)],
        (returned, partial),
        aliases={1: 1},
        name="root_sum",
    )
    root_other = swapped(root_mine, "row", 0)
    partial = call(
        expand_kernel,
        shape((rows, columns), f32),
        (partial, expand, returned),
        flops=2 * rows * expand.shape[1] * columns,
        name="expand",
    )
    return call(
        final_kernel,
        shape((rows, columns), f32),
        (partial, root_expand, root_mine, root_other),
        scratch=[pltpu.VMEM((rank, columns), bf16)],
        flops=2 * rows * rank * columns,
        name="final",
    )


def solution(mesh):
    leaves = P(("row", "col"), None)
    levels = P(None, ("row", "col"), None)
    return jax.shard_map(
        per_device,
        mesh=mesh,
        in_specs=(leaves,) * 5 + (levels,) * 2 + (leaves,) * 2 + (P(),),
        out_specs=leaves,
        check_vma=False,
    )
```

```python
import jax
import jax.numpy as jnp
from jax import lax
from jax.experimental import pallas as pl
from jax.experimental.pallas import tpu as pltpu
from jax.sharding import PartitionSpec as P

bf16 = jnp.bfloat16
f32 = jnp.float32
contract_first = (((0,), (0,)), ((), ()))
plain = (((1,), (0,)), ((), ()))
in_vmem = pl.BlockSpec(memory_space=pltpu.VMEM)
in_smem = pl.BlockSpec(memory_space=pltpu.SMEM)
in_hbm = pl.BlockSpec(memory_space=pltpu.HBM)
in_place = pl.BlockSpec(memory_space=pl.ANY)
limit = 24 * 1024 * 1024
waited = 10**10


def swapped(x, axis, bit):
    return lax.ppermute(x, axis, [(i, i ^ 1 << bit) for i in range(lax.axis_size(axis))])


out_order = (4, 2, 0, 7, 5, 3, 1, 6)
back_order = (4, 2, 0, 7, 5, 3, 1, 6)


def slots(order, count):
    parts = len(order)
    if count % parts:
        return list(range(count))
    block = count // parts
    return [part * block + i for part in order for i in range(block)]


def slot_of(order, device, count):
    return sum(jnp.where(device == d, i, 0) for i, d in enumerate(slots(order, count)))


def exchanged(x, order):
    groups = [slots(order, lax.axis_size("col"))]
    return lax.all_to_all(x, "col", 0, 0, tiled=True, axis_index_groups=groups)


def ahead(x):
    return pltpu.with_memory_space_constraint(x, pltpu.VMEM)


def left(x):
    return pltpu.with_memory_space_constraint(x, pltpu.HBM)


def mul(a, b, dims=plain):
    return lax.dot_general(a, b, dims, preferred_element_type=f32)


def shape(dims, dtype):
    return jax.ShapeDtypeStruct(dims, dtype)


def call(kernel, out, args, specs=None, out_specs=None, scratch=(), aliases=None, flops=0, name=None):
    return pl.pallas_call(
        kernel,
        out_shape=out,
        in_specs=specs or [in_vmem] * len(args),
        out_specs=out_specs or jax.tree.map(lambda _: in_vmem, out),
        scratch_shapes=scratch,
        input_output_aliases=aliases or {},
        compiler_params=pltpu.CompilerParams(vmem_limit_bytes=limit),
        cost_estimate=pl.CostEstimate(flops=flops, bytes_accessed=flops // 256, transcendentals=0),
        name=name,
    )(*args)


def compress_kernel(
    owner_hbm, x_hbm, compress_hbm, root_hbm,
    low_ref, out_hbm, send_ref, keep_ref,
    owner_ref, x_ref, compress_ref, root_ref, product_ref, out_ref, sems, compress_sems, out_sems,
):
    pieces, size, _ = out_ref.shape
    blocks = compress_sems.shape[0]
    count = pieces // blocks
    width = count * size
    x_copy = pltpu.make_async_copy(x_hbm, x_ref, sems.at[0])
    owner_copy = pltpu.make_async_copy(owner_hbm, owner_ref, sems.at[1])
    root_copy = pltpu.make_async_copy(root_hbm, root_ref, sems.at[2])
    compress_copies = [
        pltpu.make_async_copy(
            compress_hbm.at[:, b * width : (b + 1) * width],
            compress_ref.at[:, b * width : (b + 1) * width],
            compress_sems.at[b],
        )
        for b in range(blocks)
    ]
    for copy in [x_copy, owner_copy, *compress_copies, root_copy]:
        copy.start()
    x_copy.wait()
    low_ref[...] = x_ref[...].astype(bf16)
    low = low_ref[...]
    flat = low.T
    owner_copy.wait()
    outs = []
    for b in range(blocks):
        compress_copies[b].wait()
        product = mul(flat, compress_ref[:, b * width : (b + 1) * width]).astype(bf16).T
        out_ref[b * count : (b + 1) * count] = product.reshape(count, size, -1)
        for k in range(b * count, (b + 1) * count):
            outs.append(
                pltpu.make_async_copy(out_ref.at[k], out_hbm.at[slot_of(out_order, owner_ref[k], pieces)], out_sems.at[k])
            )
            outs[-1].start()
    root_copy.wait()
    product_ref[...] = mul(root_ref[...], low, contract_first)
    half = keep_ref.shape[0]
    mine = lax.rem(lax.axis_index("row"), 2)
    keep_ref[...] = product_ref[pl.ds(pl.multiple_of(mine * half, half), half), :]
    send_ref[...] = product_ref[pl.ds(pl.multiple_of((1 - mine) * half, half), half), :]
    for copy in outs:
        copy.wait()


def compressed(owner_map, x, compress, root_project):
    rows, columns = x.shape
    wide = compress.shape[1]
    pieces = owner_map.shape[0]
    rank = root_project.shape[1]
    outgoing = (pieces, wide // pieces, columns)
    return call(
        compress_kernel,
        [
            shape((rows, columns), bf16),
            shape(outgoing, bf16),
            shape((rank // 2, columns), f32),
            shape((rank // 2, columns), f32),
        ],
        (left(owner_map), left(x), left(compress), left(root_project)),
        specs=[in_place] * 4,
        out_specs=[in_vmem, in_hbm, in_vmem, in_vmem],
        scratch=[
            pltpu.SMEM(owner_map.shape, jnp.int32),
            pltpu.VMEM((rows, columns), f32),
            pltpu.VMEM((rows, wide), bf16),
            pltpu.VMEM((rows, rank), bf16),
            pltpu.VMEM((rank, columns), f32),
            pltpu.VMEM(outgoing, bf16),
            pltpu.SemaphoreType.DMA((3,)),
            pltpu.SemaphoreType.DMA((2,)),
            pltpu.SemaphoreType.DMA((pieces,)),
        ],
        flops=2 * rows * (wide + rank) * columns,
        name="compress",
    )


def split_kernel(keep_ref, got_ref, low_ref, own_ref, same_ref, other_ref, through_ref, total_ref):
    total_ref[...] = keep_ref[...] + got_ref[...].astype(f32)
    part = own_ref.shape[0]
    mine = lax.rem(lax.axis_index("col"), 2)
    own = total_ref[pl.ds(pl.multiple_of(mine * part, part), part), :]
    own_ref[...] = own
    same_ref[...] = own.astype(bf16)
    other_ref[...] = total_ref[pl.ds(pl.multiple_of((1 - mine) * part, part), part), :].astype(bf16)


def levels_kernel(low_ref, basis_hbm, out_ref, send_ref, basis_ref, sem):
    copy = pltpu.make_async_copy(basis_hbm, basis_ref, sem)
    copy.start()
    low = low_ref[...]
    copy.wait()
    for level in range(basis_ref.shape[0]):
        product = mul(basis_ref[level], low, contract_first)
        out_ref[level] = product
        send_ref[level] = product.astype(bf16)


def middle_kernel(middle_ref, arrived_ref, low_ref, running_ref, own_ref, *refs):
    got, (out_hbm, _, _, out_ref, sems) = refs[:-5], refs[-5:]
    pieces, size, columns = arrived_ref.shape
    total = own_ref[...]
    for got_ref in got:
        total += got_ref[...].astype(f32)
    part = total.astype(bf16)
    order = slots(out_order, pieces)
    back = slots(back_order, pieces)
    arrived = jnp.concatenate([arrived_ref[order.index(c)] for c in range(pieces)], axis=0)
    copies = []
    for k in range(pieces):
        out_ref[k, :size] = mul(middle_ref[k * size : (k + 1) * size, :], arrived).astype(bf16)
        out_ref[k, size:] = part
        copies.append(pltpu.make_async_copy(out_ref.at[k], out_hbm.at[back.index(k)], sems.at[k]))
        copies[-1].start()
    for copy in copies:
        copy.wait()


def add_kernel(keep_ref, got_ref, send_ref, *sum_ref):
    total = keep_ref[1:] + got_ref[1:].astype(f32)
    send_ref[...] = total.astype(bf16)
    if sum_ref:
        sum_ref[0][...] = total


def dense_kernel(
    owner_hbm, low_ref, inverse_hbm, row_hbm, expand_hbm, root_hbm,
    out_ref, row_ref, expand_ref, root_ref,
    owner_ref, inverse_ref, sems, expand_sems,
):
    owner_copy = pltpu.make_async_copy(owner_hbm, owner_ref, sems.at[0])
    inverse_copy = pltpu.make_async_copy(inverse_hbm, inverse_ref, sems.at[1])
    row_copy = pltpu.make_async_copy(row_hbm, row_ref, sems.at[2])
    root_copy = pltpu.make_async_copy(root_hbm, root_ref, sems.at[3])
    for copy in (owner_copy, inverse_copy, row_copy, root_copy):
        copy.start()
    owner_copy.wait()
    pieces = expand_sems.shape[0]
    size = expand_ref.shape[1] // pieces
    expand_copies = []
    for k in range(pieces):
        place = pl.ds(pl.multiple_of(slot_of(back_order, owner_ref[k], pieces) * size, size), size)
        expand_copies.append(
            pltpu.make_async_copy(
                expand_hbm.at[:, k * size : (k + 1) * size], expand_ref.at[:, place], expand_sems.at[k]
            )
        )
        expand_copies[-1].start()
    inverse_copy.wait()
    out_ref[...] = mul(inverse_ref[...], low_ref[...])
    for copy in (row_copy, root_copy, *expand_copies):
        copy.wait()


def couple_kernel(dense_ref, expand_ref, *refs):
    out_ref = refs[-1]
    total = dense_ref[...]
    for level, sibling_ref in enumerate(refs[:-1]):
        total += mul(expand_ref[level], sibling_ref[0])
    out_ref[...] = total


def root_kernel(returned_ref, partial_ref, out_ref, through_ref):
    part = out_ref.shape[0] // 2
    size = returned_ref.shape[1] - part
    order = slots(back_order, returned_ref.shape[0])
    for parity in range(2):
        total = jnp.zeros((part, out_ref.shape[1]), f32)
        for k in range(returned_ref.shape[0]):
            if order[k] % 2 == parity:
                total += returned_ref[k, size:, :].astype(f32)
        out_ref[parity * part : (parity + 1) * part] = total.astype(bf16)


def half_of(root_expand_ref, rows, which):
    half = rows.shape[0]
    return mul(root_expand_ref[:, pl.ds(pl.multiple_of(which * half, half), half)], rows)


def expand_kernel(partial_ref, expand_ref, returned_ref, root_expand_ref, mine_ref, out_ref):
    pieces = returned_ref.shape[0]
    size = expand_ref.shape[1] // pieces
    returned = jnp.concatenate([returned_ref[k, :size] for k in range(pieces)], axis=0)
    mine = lax.rem(lax.axis_index("row"), 2)
    out_ref[...] = (
        partial_ref[...]
        + mul(expand_ref[...], returned)
        + half_of(root_expand_ref, mine_ref[...], mine)
    )


def final_kernel(partial_ref, root_expand_ref, other_ref, out_ref):
    mine = lax.rem(lax.axis_index("row"), 2)
    out_ref[...] = partial_ref[...] + half_of(root_expand_ref, other_ref[...], 1 - mine)


def per_device(
    right_side,
    leaf_inverse,
    compress,
    middle,
    expand,
    row_project,
    row_expand,
    root_project,
    root_expand,
    owner_map,
):
    rows, columns = right_side.shape
    levels, _, rank = row_project.shape
    row_count = lax.axis_size("row")
    col_count = lax.axis_size("col")
    half = rank // 2
    part = half // 2

    low, outgoing, send, keep = compressed(owner_map, right_side, compress, root_project)
    got = swapped(send, "row", 0)
    arrived = exchanged(outgoing, out_order)
    own, same, other, low = call(
        split_kernel,
        [
            shape((part, columns), f32),
            shape((part, columns), bf16),
            shape((part, columns), bf16),
            shape(low.shape, bf16),
        ],
        (keep, got, low),
        scratch=[pltpu.VMEM((half, columns), f32)],
        aliases={2: 3},
        flops=waited,
        name="root_split",
    )
    parts = []
    for row_step in range(0, row_count, 2):
        for col_step in range(2):
            if row_step or col_step:
                pairs = [
                    (r * col_count + c, (r ^ row_step) * col_count + (c ^ col_step))
                    for r in range(row_count)
                    for c in range(col_count)
                ]
                parts.append(lax.ppermute(other if col_step else same, ("row", "col"), pairs))
    running, level_send = call(
        levels_kernel,
        [shape((levels, rank, columns), f32), shape((levels, rank, columns), bf16)],
        (low, left(row_project)),
        specs=[in_vmem, in_place],
        scratch=[pltpu.VMEM(row_project.shape, bf16), pltpu.SemaphoreType.DMA],
        flops=2 * rows * rank * levels * columns,
        name="levels",
    )
    partner = swapped(level_send, "row", 0)

    size = middle.shape[0] // col_count
    mixed_shape = (col_count, size + part, columns)
    mixed, low, running = call(
        middle_kernel,
        [shape(mixed_shape, bf16), shape(low.shape, bf16), shape(running.shape, f32)],
        (ahead(middle), arrived, low, running, own, *parts),
        out_specs=[in_hbm, in_vmem, in_vmem],
        scratch=[pltpu.VMEM(mixed_shape, bf16), pltpu.SemaphoreType.DMA((col_count,))],
        aliases={2: 1, 3: 2},
        flops=2 * middle.shape[0] * middle.shape[1] * columns,
        name="middle",
    )
    returned = exchanged(mixed, back_order)

    dense, row_expand, expand, root_expand = call(
        dense_kernel,
        [
            shape((rows, columns), f32),
            pltpu.VMEM(row_expand.shape, bf16),
            pltpu.VMEM(expand.shape, bf16),
            pltpu.VMEM(root_expand.shape, bf16),
        ],
        (left(owner_map), low, left(leaf_inverse), left(row_expand), left(expand), left(root_expand)),
        specs=[in_place, in_vmem] + [in_place] * 4,
        scratch=[
            pltpu.SMEM(owner_map.shape, jnp.int32),
            pltpu.VMEM(leaf_inverse.shape, bf16),
            pltpu.SemaphoreType.DMA((4,)),
            pltpu.SemaphoreType.DMA((col_count,)),
        ],
        flops=2 * rows * rows * columns,
        name="dense",
    )
    siblings = [partner]
    for bit in range(1, levels):
        dims = (levels - bit, rank, columns)
        out = [shape(dims, bf16)] + [shape(dims, f32)] * (bit + 1 < levels)
        level_send, *running = call(add_kernel, out, (running, partner), name="level_sum")
        running = running[0] if running else None
        partner = swapped(level_send, "row", bit)
        siblings.append(partner)
    partial = call(
        couple_kernel,
        shape((rows, columns), f32),
        (dense, row_expand, *siblings),
        flops=2 * rows * rank * levels * columns,
        name="couple",
    )

    root_mine, partial = call(
        root_kernel,
        [shape((half, columns), bf16), shape(partial.shape, f32)],
        (returned, partial),
        aliases={1: 1},
        name="root_sum",
    )
    root_other = swapped(root_mine, "row", 0)
    partial = call(
        expand_kernel,
        shape((rows, columns), f32),
        (partial, expand, returned, root_expand, root_mine),
        flops=2 * rows * expand.shape[1] * columns,
        name="expand",
    )
    return call(
        final_kernel,
        shape((rows, columns), f32),
        (partial, root_expand, root_other),
        flops=2 * rows * rank * columns,
        name="final",
    )


def solution(mesh):
    leaves = P(("row", "col"), None)
    levels = P(None, ("row", "col"), None)
    return jax.shard_map(
        per_device,
        mesh=mesh,
        in_specs=(leaves,) * 5 + (levels,) * 2 + (leaves,) * 2 + (P(),),
        out_specs=leaves,
        check_vma=False,
    )
```

```python
import jax
import jax.numpy as jnp
from jax import lax
from jax.experimental import pallas as pl
from jax.experimental.pallas import tpu as pltpu
from jax.sharding import PartitionSpec as P

bf16 = jnp.bfloat16
f32 = jnp.float32
contract_first = (((0,), (0,)), ((), ()))
plain = (((1,), (0,)), ((), ()))
in_vmem = pl.BlockSpec(memory_space=pltpu.VMEM)
in_smem = pl.BlockSpec(memory_space=pltpu.SMEM)
in_hbm = pl.BlockSpec(memory_space=pltpu.HBM)
in_place = pl.BlockSpec(memory_space=pl.ANY)
limit = 24 * 1024 * 1024
waited = 10**10


def swapped(x, axis, bit):
    return lax.ppermute(x, axis, [(i, i ^ 1 << bit) for i in range(lax.axis_size(axis))])


out_order = (4, 2, 0, 7, 5, 3, 1, 6)
back_order = (4, 2, 0, 7, 5, 3, 1, 6)


def slots(order, count):
    parts = len(order)
    if count % parts:
        return list(range(count))
    block = count // parts
    return [part * block + i for part in order for i in range(block)]


def slot_of(order, device, count):
    return sum(jnp.where(device == d, i, 0) for i, d in enumerate(slots(order, count)))


def exchanged(x, order):
    groups = [slots(order, lax.axis_size("col"))]
    return lax.all_to_all(x, "col", 0, 0, tiled=True, axis_index_groups=groups)


def ahead(x):
    return pltpu.with_memory_space_constraint(x, pltpu.VMEM)


def left(x):
    return pltpu.with_memory_space_constraint(x, pltpu.HBM)


def mul(a, b, dims=plain):
    return lax.dot_general(a, b, dims, preferred_element_type=f32)


def shape(dims, dtype):
    return jax.ShapeDtypeStruct(dims, dtype)


def call(kernel, out, args, specs=None, out_specs=None, scratch=(), aliases=None, flops=0, name=None):
    return pl.pallas_call(
        kernel,
        out_shape=out,
        in_specs=specs or [in_vmem] * len(args),
        out_specs=out_specs or jax.tree.map(lambda _: in_vmem, out),
        scratch_shapes=scratch,
        input_output_aliases=aliases or {},
        compiler_params=pltpu.CompilerParams(vmem_limit_bytes=limit),
        cost_estimate=pl.CostEstimate(flops=flops, bytes_accessed=flops // 256, transcendentals=0),
        name=name,
    )(*args)


def compress_kernel(
    owner_hbm, x_hbm, compress_hbm, root_hbm,
    low_ref, out_hbm, send_ref, keep_ref,
    owner_ref, x_ref, compress_ref, root_ref, product_ref, out_ref, sems, compress_sems, out_sems,
):
    pieces, size, _ = out_ref.shape
    blocks = compress_sems.shape[0]
    count = pieces // blocks
    width = count * size
    x_copy = pltpu.make_async_copy(x_hbm, x_ref, sems.at[0])
    owner_copy = pltpu.make_async_copy(owner_hbm, owner_ref, sems.at[1])
    root_copy = pltpu.make_async_copy(root_hbm, root_ref, sems.at[2])
    compress_copies = [
        pltpu.make_async_copy(
            compress_hbm.at[:, b * width : (b + 1) * width],
            compress_ref.at[:, b * width : (b + 1) * width],
            compress_sems.at[b],
        )
        for b in range(blocks)
    ]
    for copy in [x_copy, owner_copy, *compress_copies, root_copy]:
        copy.start()
    x_copy.wait()
    low_ref[...] = x_ref[...].astype(bf16)
    low = low_ref[...]
    flat = low.T
    owner_copy.wait()
    outs = []
    for b in range(blocks):
        compress_copies[b].wait()
        product = mul(flat, compress_ref[:, b * width : (b + 1) * width]).astype(bf16).T
        out_ref[b * count : (b + 1) * count] = product.reshape(count, size, -1)
        for k in range(b * count, (b + 1) * count):
            outs.append(
                pltpu.make_async_copy(out_ref.at[k], out_hbm.at[slot_of(out_order, owner_ref[k], pieces)], out_sems.at[k])
            )
            outs[-1].start()
    root_copy.wait()
    product_ref[...] = mul(root_ref[...], low, contract_first)
    half = keep_ref.shape[0]
    mine = lax.rem(lax.axis_index("row"), 2)
    keep_ref[...] = product_ref[pl.ds(pl.multiple_of(mine * half, half), half), :]
    send_ref[...] = product_ref[pl.ds(pl.multiple_of((1 - mine) * half, half), half), :]
    for copy in outs:
        copy.wait()


def compressed(owner_map, x, compress, root_project):
    rows, columns = x.shape
    wide = compress.shape[1]
    pieces = owner_map.shape[0]
    rank = root_project.shape[1]
    outgoing = (pieces, wide // pieces, columns)
    return call(
        compress_kernel,
        [
            shape((rows, columns), bf16),
            shape(outgoing, bf16),
            shape((rank // 2, columns), f32),
            shape((rank // 2, columns), f32),
        ],
        (left(owner_map), left(x), left(compress), left(root_project)),
        specs=[in_place] * 4,
        out_specs=[in_vmem, in_hbm, in_vmem, in_vmem],
        scratch=[
            pltpu.SMEM(owner_map.shape, jnp.int32),
            pltpu.VMEM((rows, columns), f32),
            pltpu.VMEM((rows, wide), bf16),
            pltpu.VMEM((rows, rank), bf16),
            pltpu.VMEM((rank, columns), f32),
            pltpu.VMEM(outgoing, bf16),
            pltpu.SemaphoreType.DMA((3,)),
            pltpu.SemaphoreType.DMA((2,)),
            pltpu.SemaphoreType.DMA((pieces,)),
        ],
        flops=2 * rows * (wide + rank) * columns,
        name="compress",
    )


def split_kernel(keep_ref, got_ref, low_ref, own_ref, same_ref, other_ref, through_ref, total_ref):
    total_ref[...] = keep_ref[...] + got_ref[...].astype(f32)
    part = own_ref.shape[0]
    mine = lax.rem(lax.axis_index("col"), 2)
    own = total_ref[pl.ds(pl.multiple_of(mine * part, part), part), :]
    own_ref[...] = own
    same_ref[...] = own.astype(bf16)
    other_ref[...] = total_ref[pl.ds(pl.multiple_of((1 - mine) * part, part), part), :].astype(bf16)


def levels_kernel(low_ref, basis_hbm, out_ref, send_ref, basis_ref, sem):
    copy = pltpu.make_async_copy(basis_hbm, basis_ref, sem)
    copy.start()
    low = low_ref[...]
    copy.wait()
    for level in range(basis_ref.shape[0]):
        product = mul(basis_ref[level], low, contract_first)
        out_ref[level] = product
        send_ref[level] = product.astype(bf16)


def middle_kernel(middle_ref, arrived_ref, low_ref, running_ref, own_ref, *refs):
    got, (out_hbm, _, _, out_ref, sems) = refs[:-5], refs[-5:]
    pieces, size, columns = arrived_ref.shape
    total = own_ref[...]
    for got_ref in got:
        total += got_ref[...].astype(f32)
    part = total.astype(bf16)
    order = slots(out_order, pieces)
    back = slots(back_order, pieces)
    arrived = jnp.concatenate([arrived_ref[order.index(c)] for c in range(pieces)], axis=0)
    copies = []
    for first in range(0, pieces, 2):
        product = mul(middle_ref[first * size : (first + 2) * size, :], arrived).astype(bf16)
        for k in range(first, first + 2):
            out_ref[k, :size] = product[(k - first) * size : (k - first + 1) * size]
            out_ref[k, size:] = part
            copies.append(pltpu.make_async_copy(out_ref.at[k], out_hbm.at[back.index(k)], sems.at[k]))
            copies[-1].start()
    for copy in copies:
        copy.wait()


def add_kernel(keep_ref, got_ref, send_ref, *sum_ref):
    total = keep_ref[1:] + got_ref[1:].astype(f32)
    send_ref[...] = total.astype(bf16)
    if sum_ref:
        sum_ref[0][...] = total


def dense_kernel(
    owner_hbm, low_ref, inverse_hbm, expand_hbm,
    out_ref, expand_ref,
    owner_ref, inverse_ref, sems, expand_sems,
):
    owner_copy = pltpu.make_async_copy(owner_hbm, owner_ref, sems.at[0])
    inverse_copy = pltpu.make_async_copy(inverse_hbm, inverse_ref, sems.at[1])
    owner_copy.start()
    inverse_copy.start()
    owner_copy.wait()
    pieces = expand_sems.shape[0]
    size = expand_ref.shape[1] // pieces
    expand_copies = []
    for k in range(pieces):
        place = pl.ds(pl.multiple_of(slot_of(back_order, owner_ref[k], pieces) * size, size), size)
        expand_copies.append(
            pltpu.make_async_copy(
                expand_hbm.at[:, k * size : (k + 1) * size], expand_ref.at[:, place], expand_sems.at[k]
            )
        )
        expand_copies[-1].start()
    inverse_copy.wait()
    out_ref[...] = mul(inverse_ref[...], low_ref[...])
    for copy in expand_copies:
        copy.wait()


def couple_kernel(dense_ref, expand_ref, *refs):
    out_ref = refs[-1]
    total = dense_ref[...]
    for level, sibling_ref in enumerate(refs[:-1]):
        total += mul(expand_ref[level], sibling_ref[0])
    out_ref[...] = total


def root_kernel(returned_ref, partial_ref, out_ref, through_ref):
    part = out_ref.shape[0] // 2
    size = returned_ref.shape[1] - part
    order = slots(back_order, returned_ref.shape[0])
    for parity in range(2):
        total = jnp.zeros((part, out_ref.shape[1]), f32)
        for k in range(returned_ref.shape[0]):
            if order[k] % 2 == parity:
                total += returned_ref[k, size:, :].astype(f32)
        out_ref[parity * part : (parity + 1) * part] = total.astype(bf16)


def half_of(root_expand_ref, rows, which):
    half = rows.shape[0]
    return mul(root_expand_ref[:, pl.ds(pl.multiple_of(which * half, half), half)], rows)


def expand_kernel(partial_ref, expand_ref, returned_ref, root_expand_ref, mine_ref, out_ref):
    pieces = returned_ref.shape[0]
    size = expand_ref.shape[1] // pieces
    returned = jnp.concatenate([returned_ref[k, :size] for k in range(pieces)], axis=0)
    mine = lax.rem(lax.axis_index("row"), 2)
    out_ref[...] = (
        partial_ref[...]
        + mul(expand_ref[...], returned)
        + half_of(root_expand_ref, mine_ref[...], mine)
    )


def final_kernel(partial_ref, root_expand_ref, other_ref, out_ref):
    mine = lax.rem(lax.axis_index("row"), 2)
    out_ref[...] = partial_ref[...] + half_of(root_expand_ref, other_ref[...], 1 - mine)


def per_device(
    right_side,
    leaf_inverse,
    compress,
    middle,
    expand,
    row_project,
    row_expand,
    root_project,
    root_expand,
    owner_map,
):
    rows, columns = right_side.shape
    levels, _, rank = row_project.shape
    row_count = lax.axis_size("row")
    col_count = lax.axis_size("col")
    half = rank // 2
    part = half // 2

    low, outgoing, send, keep = compressed(owner_map, right_side, compress, root_project)
    got = swapped(send, "row", 0)
    arrived = exchanged(outgoing, out_order)
    own, same, other, low = call(
        split_kernel,
        [
            shape((part, columns), f32),
            shape((part, columns), bf16),
            shape((part, columns), bf16),
            shape(low.shape, bf16),
        ],
        (keep, got, low),
        scratch=[pltpu.VMEM((half, columns), f32)],
        aliases={2: 3},
        flops=waited,
        name="root_split",
    )
    parts = []
    for row_step in range(0, row_count, 2):
        for col_step in range(2):
            if row_step or col_step:
                pairs = [
                    (r * col_count + c, (r ^ row_step) * col_count + (c ^ col_step))
                    for r in range(row_count)
                    for c in range(col_count)
                ]
                parts.append(lax.ppermute(other if col_step else same, ("row", "col"), pairs))
    running, level_send = call(
        levels_kernel,
        [shape((levels, rank, columns), f32), shape((levels, rank, columns), bf16)],
        (low, left(row_project)),
        specs=[in_vmem, in_place],
        scratch=[pltpu.VMEM(row_project.shape, bf16), pltpu.SemaphoreType.DMA],
        flops=2 * rows * rank * levels * columns,
        name="levels",
    )
    partner = swapped(level_send, "row", 0)

    size = middle.shape[0] // col_count
    mixed_shape = (col_count, size + part, columns)
    mixed, low, running = call(
        middle_kernel,
        [shape(mixed_shape, bf16), shape(low.shape, bf16), shape(running.shape, f32)],
        (ahead(middle), arrived, low, running, own, *parts),
        out_specs=[in_hbm, in_vmem, in_vmem],
        scratch=[pltpu.VMEM(mixed_shape, bf16), pltpu.SemaphoreType.DMA((col_count,))],
        aliases={2: 1, 3: 2},
        flops=2 * middle.shape[0] * middle.shape[1] * columns,
        name="middle",
    )
    returned = exchanged(mixed, back_order)

    dense, expand = call(
        dense_kernel,
        [
            shape((rows, columns), f32),
            pltpu.VMEM(expand.shape, bf16),
        ],
        (left(owner_map), low, left(leaf_inverse), left(expand)),
        specs=[in_place, in_vmem] + [in_place] * 2,
        scratch=[
            pltpu.SMEM(owner_map.shape, jnp.int32),
            pltpu.VMEM(leaf_inverse.shape, bf16),
            pltpu.SemaphoreType.DMA((2,)),
            pltpu.SemaphoreType.DMA((col_count,)),
        ],
        flops=2 * rows * rows * columns,
        name="dense",
    )
    siblings = [partner]
    for bit in range(1, levels):
        dims = (levels - bit, rank, columns)
        out = [shape(dims, bf16)] + [shape(dims, f32)] * (bit + 1 < levels)
        level_send, *running = call(add_kernel, out, (running, partner), name="level_sum")
        running = running[0] if running else None
        partner = swapped(level_send, "row", bit)
        siblings.append(partner)
    partial = call(
        couple_kernel,
        shape((rows, columns), f32),
        (dense, ahead(row_expand), *siblings),
        flops=2 * rows * rank * levels * columns,
        name="couple",
    )

    root_mine, partial = call(
        root_kernel,
        [shape((half, columns), bf16), shape(partial.shape, f32)],
        (returned, partial),
        aliases={1: 1},
        name="root_sum",
    )
    root_other = swapped(root_mine, "row", 0)
    partial = call(
        expand_kernel,
        shape((rows, columns), f32),
        (partial, expand, returned, ahead(root_expand), root_mine),
        flops=2 * rows * expand.shape[1] * columns,
        name="expand",
    )
    return call(
        final_kernel,
        shape((rows, columns), f32),
        (partial, ahead(root_expand), root_other),
        flops=2 * rows * rank * columns,
        name="final",
    )


def solution(mesh):
    leaves = P(("row", "col"), None)
    levels = P(None, ("row", "col"), None)
    return jax.shard_map(
        per_device,
        mesh=mesh,
        in_specs=(leaves,) * 5 + (levels,) * 2 + (leaves,) * 2 + (P(),),
        out_specs=leaves,
        check_vma=False,
    )
```

```python
import jax
import jax.numpy as jnp
from jax import lax
from jax.experimental import pallas as pl
from jax.experimental.pallas import tpu as pltpu
from jax.sharding import PartitionSpec as P

bf16 = jnp.bfloat16
f32 = jnp.float32
contract_first = (((0,), (0,)), ((), ()))
plain = (((1,), (0,)), ((), ()))
in_vmem = pl.BlockSpec(memory_space=pltpu.VMEM)
in_smem = pl.BlockSpec(memory_space=pltpu.SMEM)
in_hbm = pl.BlockSpec(memory_space=pltpu.HBM)
in_place = pl.BlockSpec(memory_space=pl.ANY)
limit = 24 * 1024 * 1024
waited = 10**10


def swapped(x, axis, bit):
    return lax.ppermute(x, axis, [(i, i ^ 1 << bit) for i in range(lax.axis_size(axis))])


out_order = (4, 2, 0, 7, 5, 3, 1, 6)
back_order = (4, 2, 0, 7, 5, 3, 1, 6)


def slots(order, count):
    parts = len(order)
    if count % parts:
        return list(range(count))
    block = count // parts
    return [part * block + i for part in order for i in range(block)]


def slot_of(order, device, count):
    return sum(jnp.where(device == d, i, 0) for i, d in enumerate(slots(order, count)))


def exchanged(x, order):
    groups = [slots(order, lax.axis_size("col"))]
    return lax.all_to_all(x, "col", 0, 0, tiled=True, axis_index_groups=groups)


def ahead(x):
    return pltpu.with_memory_space_constraint(x, pltpu.VMEM)


def left(x):
    return pltpu.with_memory_space_constraint(x, pltpu.HBM)


def mul(a, b, dims=plain):
    return lax.dot_general(a, b, dims, preferred_element_type=f32)


def shape(dims, dtype):
    return jax.ShapeDtypeStruct(dims, dtype)


def call(kernel, out, args, specs=None, out_specs=None, scratch=(), aliases=None, flops=0, name=None):
    return pl.pallas_call(
        kernel,
        out_shape=out,
        in_specs=specs or [in_vmem] * len(args),
        out_specs=out_specs or jax.tree.map(lambda _: in_vmem, out),
        scratch_shapes=scratch,
        input_output_aliases=aliases or {},
        compiler_params=pltpu.CompilerParams(vmem_limit_bytes=limit),
        cost_estimate=pl.CostEstimate(flops=flops, bytes_accessed=flops // 256, transcendentals=0),
        name=name,
    )(*args)


def compress_kernel(
    owner_hbm, x_hbm, compress_hbm, root_hbm,
    low_ref, out_hbm, send_ref, keep_ref,
    owner_ref, x_ref, compress_ref, root_ref, product_ref, out_ref, sems, compress_sems, out_sems,
):
    pieces, size, _ = out_ref.shape
    blocks = compress_sems.shape[0]
    count = pieces // blocks
    width = count * size
    x_copy = pltpu.make_async_copy(x_hbm, x_ref, sems.at[0])
    owner_copy = pltpu.make_async_copy(owner_hbm, owner_ref, sems.at[1])
    root_copy = pltpu.make_async_copy(root_hbm, root_ref, sems.at[2])
    compress_copies = [
        pltpu.make_async_copy(
            compress_hbm.at[:, b * width : (b + 1) * width],
            compress_ref.at[:, b * width : (b + 1) * width],
            compress_sems.at[b],
        )
        for b in range(blocks)
    ]
    for copy in [x_copy, owner_copy, *compress_copies, root_copy]:
        copy.start()
    x_copy.wait()
    low_ref[...] = x_ref[...].astype(bf16)
    low = low_ref[...]
    flat = low.T
    owner_copy.wait()
    outs = []
    for b in range(blocks):
        compress_copies[b].wait()
        product = mul(flat, compress_ref[:, b * width : (b + 1) * width]).astype(bf16).T
        out_ref[b * count : (b + 1) * count] = product.reshape(count, size, -1)
        for k in range(b * count, (b + 1) * count):
            outs.append(
                pltpu.make_async_copy(out_ref.at[k], out_hbm.at[slot_of(out_order, owner_ref[k], pieces)], out_sems.at[k])
            )
            outs[-1].start()
    root_copy.wait()
    product_ref[...] = mul(root_ref[...], low, contract_first)
    half = keep_ref.shape[0]
    mine = lax.rem(lax.axis_index("row"), 2)
    keep_ref[...] = product_ref[pl.ds(pl.multiple_of(mine * half, half), half), :]
    send_ref[...] = product_ref[pl.ds(pl.multiple_of((1 - mine) * half, half), half), :]
    for copy in outs:
        copy.wait()


def compressed(owner_map, x, compress, root_project):
    rows, columns = x.shape
    wide = compress.shape[1]
    pieces = owner_map.shape[0]
    rank = root_project.shape[1]
    outgoing = (pieces, wide // pieces, columns)
    return call(
        compress_kernel,
        [
            shape((rows, columns), bf16),
            shape(outgoing, bf16),
            shape((rank // 2, columns), f32),
            shape((rank // 2, columns), f32),
        ],
        (left(owner_map), left(x), left(compress), left(root_project)),
        specs=[in_place] * 4,
        out_specs=[in_vmem, in_hbm, in_vmem, in_vmem],
        scratch=[
            pltpu.SMEM(owner_map.shape, jnp.int32),
            pltpu.VMEM((rows, columns), f32),
            pltpu.VMEM((rows, wide), bf16),
            pltpu.VMEM((rows, rank), bf16),
            pltpu.VMEM((rank, columns), f32),
            pltpu.VMEM(outgoing, bf16),
            pltpu.SemaphoreType.DMA((3,)),
            pltpu.SemaphoreType.DMA((2,)),
            pltpu.SemaphoreType.DMA((pieces,)),
        ],
        flops=2 * rows * (wide + rank) * columns,
        name="compress",
    )


def split_kernel(keep_ref, got_ref, low_ref, own_ref, same_ref, other_ref, through_ref, total_ref):
    total_ref[...] = keep_ref[...] + got_ref[...].astype(f32)
    part = own_ref.shape[0]
    mine = lax.rem(lax.axis_index("col"), 2)
    own = total_ref[pl.ds(pl.multiple_of(mine * part, part), part), :]
    own_ref[...] = own
    same_ref[...] = own.astype(bf16)
    other_ref[...] = total_ref[pl.ds(pl.multiple_of((1 - mine) * part, part), part), :].astype(bf16)


def levels_kernel(low_ref, basis_hbm, out_ref, send_ref, basis_ref, sem):
    copy = pltpu.make_async_copy(basis_hbm, basis_ref, sem)
    copy.start()
    low = low_ref[...]
    copy.wait()
    for level in range(basis_ref.shape[0]):
        product = mul(basis_ref[level], low, contract_first)
        out_ref[level] = product
        send_ref[level] = product.astype(bf16)


def middle_kernel(middle_ref, arrived_ref, low_ref, running_ref, own_ref, *refs):
    got, (out_hbm, _, _, out_ref, sems) = refs[:-5], refs[-5:]
    pieces, size, columns = arrived_ref.shape
    total = own_ref[...]
    for got_ref in got:
        total += got_ref[...].astype(f32)
    part = total.astype(bf16)
    order = slots(out_order, pieces)
    back = slots(back_order, pieces)
    arrived = jnp.concatenate([arrived_ref[order.index(c)] for c in range(pieces)], axis=0)
    copies = []
    for first in range(0, pieces, 2):
        product = mul(middle_ref[first * size : (first + 2) * size, :], arrived).astype(bf16)
        for k in range(first, first + 2):
            out_ref[k, :size] = product[(k - first) * size : (k - first + 1) * size]
            out_ref[k, size:] = part
            copies.append(pltpu.make_async_copy(out_ref.at[k], out_hbm.at[back.index(k)], sems.at[k]))
            copies[-1].start()
    for copy in copies:
        copy.wait()


def add_kernel(keep_ref, got_ref, send_ref, *sum_ref):
    total = keep_ref[1:] + got_ref[1:].astype(f32)
    send_ref[...] = total.astype(bf16)
    if sum_ref:
        sum_ref[0][...] = total


def dense_kernel(
    owner_hbm, low_ref, inverse_hbm, row_hbm, expand_hbm, root_hbm,
    out_ref, row_ref, expand_ref, root_ref,
    owner_ref, inverse_ref, sems, expand_sems,
):
    owner_copy = pltpu.make_async_copy(owner_hbm, owner_ref, sems.at[0])
    inverse_copy = pltpu.make_async_copy(inverse_hbm, inverse_ref, sems.at[1])
    row_copy = pltpu.make_async_copy(row_hbm, row_ref, sems.at[2])
    root_copy = pltpu.make_async_copy(root_hbm, root_ref, sems.at[3])
    for copy in (owner_copy, inverse_copy, row_copy, root_copy):
        copy.start()
    owner_copy.wait()
    pieces = expand_sems.shape[0]
    size = expand_ref.shape[1] // pieces
    expand_copies = []
    for k in range(pieces):
        place = pl.ds(pl.multiple_of(slot_of(back_order, owner_ref[k], pieces) * size, size), size)
        expand_copies.append(
            pltpu.make_async_copy(
                expand_hbm.at[:, k * size : (k + 1) * size], expand_ref.at[:, place], expand_sems.at[k]
            )
        )
        expand_copies[-1].start()
    inverse_copy.wait()
    out_ref[...] = mul(inverse_ref[...], low_ref[...])
    for copy in (row_copy, root_copy, *expand_copies):
        copy.wait()


def couple_kernel(dense_ref, expand_ref, *refs):
    out_ref = refs[-1]
    total = dense_ref[...]
    for level, sibling_ref in enumerate(refs[:-1]):
        total += mul(expand_ref[level], sibling_ref[0])
    out_ref[...] = total


def root_kernel(returned_ref, partial_ref, out_ref, through_ref):
    part = out_ref.shape[0] // 2
    size = returned_ref.shape[1] - part
    order = slots(back_order, returned_ref.shape[0])
    for parity in range(2):
        total = jnp.zeros((part, out_ref.shape[1]), f32)
        for k in range(returned_ref.shape[0]):
            if order[k] % 2 == parity:
                total += returned_ref[k, size:, :].astype(f32)
        out_ref[parity * part : (parity + 1) * part] = total.astype(bf16)


def half_of(root_expand_ref, rows, which):
    half = rows.shape[0]
    return mul(root_expand_ref[:, pl.ds(pl.multiple_of(which * half, half), half)], rows)


def expand_kernel(partial_ref, expand_ref, returned_ref, root_expand_ref, mine_ref, out_ref):
    pieces = returned_ref.shape[0]
    size = expand_ref.shape[1] // pieces
    returned = jnp.concatenate([returned_ref[k, :size] for k in range(pieces)], axis=0)
    mine = lax.rem(lax.axis_index("row"), 2)
    out_ref[...] = (
        partial_ref[...]
        + mul(expand_ref[...], returned)
        + half_of(root_expand_ref, mine_ref[...], mine)
    )


def final_kernel(partial_ref, root_expand_ref, other_ref, out_ref):
    mine = lax.rem(lax.axis_index("row"), 2)
    out_ref[...] = partial_ref[...] + half_of(root_expand_ref, other_ref[...], 1 - mine)


def per_device(
    right_side,
    leaf_inverse,
    compress,
    middle,
    expand,
    row_project,
    row_expand,
    root_project,
    root_expand,
    owner_map,
):
    rows, columns = right_side.shape
    levels, _, rank = row_project.shape
    row_count = lax.axis_size("row")
    col_count = lax.axis_size("col")
    half = rank // 2
    part = half // 2

    low, outgoing, send, keep = compressed(owner_map, right_side, compress, root_project)
    got = swapped(send, "row", 0)
    arrived = exchanged(outgoing, out_order)
    own, same, other, low = call(
        split_kernel,
        [
            shape((part, columns), f32),
            shape((part, columns), bf16),
            shape((part, columns), bf16),
            shape(low.shape, bf16),
        ],
        (keep, got, low),
        scratch=[pltpu.VMEM((half, columns), f32)],
        aliases={2: 3},
        flops=waited,
        name="root_split",
    )
    parts = []
    for row_step in range(0, row_count, 2):
        for col_step in range(2):
            if row_step or col_step:
                pairs = [
                    (r * col_count + c, (r ^ row_step) * col_count + (c ^ col_step))
                    for r in range(row_count)
                    for c in range(col_count)
                ]
                parts.append(lax.ppermute(other if col_step else same, ("row", "col"), pairs))
    running, level_send = call(
        levels_kernel,
        [shape((levels, rank, columns), f32), shape((levels, rank, columns), bf16)],
        (low, left(row_project)),
        specs=[in_vmem, in_place],
        scratch=[pltpu.VMEM(row_project.shape, bf16), pltpu.SemaphoreType.DMA],
        flops=2 * rows * rank * levels * columns,
        name="levels",
    )
    partner = swapped(level_send, "row", 0)

    size = middle.shape[0] // col_count
    mixed_shape = (col_count, size + part, columns)
    mixed, low, running = call(
        middle_kernel,
        [shape(mixed_shape, bf16), shape(low.shape, bf16), shape(running.shape, f32)],
        (ahead(middle), arrived, low, running, own, *parts),
        out_specs=[in_hbm, in_vmem, in_vmem],
        scratch=[pltpu.VMEM(mixed_shape, bf16), pltpu.SemaphoreType.DMA((col_count,))],
        aliases={2: 1, 3: 2},
        flops=2 * middle.shape[0] * middle.shape[1] * columns,
        name="middle",
    )
    returned = exchanged(mixed, back_order)

    dense, row_expand, expand, root_expand = call(
        dense_kernel,
        [
            shape((rows, columns), f32),
            pltpu.VMEM(row_expand.shape, bf16),
            pltpu.VMEM(expand.shape, bf16),
            pltpu.VMEM(root_expand.shape, bf16),
        ],
        (left(owner_map), low, left(leaf_inverse), left(row_expand), left(expand), left(root_expand)),
        specs=[in_place, in_vmem] + [in_place] * 4,
        scratch=[
            pltpu.SMEM(owner_map.shape, jnp.int32),
            pltpu.VMEM(leaf_inverse.shape, bf16),
            pltpu.SemaphoreType.DMA((4,)),
            pltpu.SemaphoreType.DMA((col_count,)),
        ],
        flops=2 * rows * rows * columns,
        name="dense",
    )
    siblings = [partner]
    for bit in range(1, levels):
        dims = (levels - bit, rank, columns)
        out = [shape(dims, bf16)] + [shape(dims, f32)] * (bit + 1 < levels)
        level_send, *running = call(add_kernel, out, (running, partner), name="level_sum")
        running = running[0] if running else None
        partner = swapped(level_send, "row", bit)
        siblings.append(partner)
    partial = call(
        couple_kernel,
        shape((rows, columns), f32),
        (dense, row_expand, *siblings),
        flops=2 * rows * rank * levels * columns,
        name="couple",
    )

    root_mine, partial = call(
        root_kernel,
        [shape((half, columns), bf16), shape(partial.shape, f32)],
        (returned, partial),
        aliases={1: 1},
        name="root_sum",
    )
    root_other = swapped(root_mine, "row", 0)
    partial = call(
        expand_kernel,
        shape((rows, columns), f32),
        (partial, expand, returned, root_expand, root_mine),
        flops=2 * rows * expand.shape[1] * columns,
        name="expand",
    )
    return call(
        final_kernel,
        shape((rows, columns), f32),
        (partial, root_expand, root_other),
        flops=2 * rows * rank * columns,
        name="final",
    )


def solution(mesh):
    leaves = P(("row", "col"), None)
    levels = P(None, ("row", "col"), None)
    return jax.shard_map(
        per_device,
        mesh=mesh,
        in_specs=(leaves,) * 5 + (levels,) * 2 + (leaves,) * 2 + (P(),),
        out_specs=leaves,
        check_vma=False,
    )
```
